32 devices in a mesh: dp: 1, expert: 32 (over z, y, x, core).
Axes of the slice: x: 2, y: 2, z: 4, core: 2. Of those that a mesh axis runs over, the one named last changes fastest.
Arguments:
- tokens: bfloat16 [4096, 3584], P('expert', 'dp'), may hold values from -6 to 6
- cotangent: bfloat16 [4096, 3584], P('expert', 'dp'), may hold values from -6 to 6
- expert_ids: int32 [4096, 4], P('expert'), may hold values from 0 to 27, all different within a row; in each aligned block of 128 rows (0 to 127, 128 to 255, ...) at most 22 rows name the same one
- gate_probs: bfloat16 [4096, 4], P('expert'), may hold values from 0.049804688 to 1
- slot_expert: int32 [32], replicated, may hold values from 0 to 27, as said below
- w_gate: bfloat16 [32, 3584, 1024], P('expert', None, 'dp'), as said below
- w_up: bfloat16 [32, 3584, 1024], P('expert', None, 'dp'), as said below
- w_down: bfloat16 [32, 1024, 3584], P('expert', 'dp'), as said below
Outputs:
- d_tokens: bfloat16 [4096, 3584], P('expert', 'dp')
- d_probs: float32 [4096, 4], P('expert')
- grad_gate: bfloat16 [32, 3584, 1024], P('expert', None, 'dp')
- grad_up: bfloat16 [32, 3584, 1024], P('expert', None, 'dp')
- grad_down: bfloat16 [32, 1024, 3584], P('expert', 'dp')
The draws below stay inside these ranges and needn't reach their ends.
Inputs may be any that keep to these rules, and one draw needn't show every extreme that they name: `expert_ids`: in each aligned block of 128 rows no expert is named by more than 22 rows, a bound that some block reaches. `slot_expert`: every expert appears once or twice; an expert that appears twice holds slots 2 j and 2 j + 1 for some j, and 4 experts appear twice. `w_gate`: slots that hold the same expert hold equal weights. `w_up`: slots that hold the same expert hold equal weights. `w_down`: slots that hold the same expert hold equal weights.
All inputs are finite; a program needn't handle non-finite values.
Results may differ from the reference program's by a relative error of at most 0.015.
Values may be sent and summed in bfloat16 or wider, within the bound.
A program may use at most 256 MiB of HBM per device.

```python
import math
import jax
import jax.numpy as jnp
import numpy as np
from jax import lax

D = 3584
HID = 1024
TOP = 4
TOK_GRP = 128
REPL = 4
SLOTS = 32
EXPERTS = 28
CAP = 22
TOKENS = 4096
N_DP = 1
N_EXPERT = 32


def placement_table(key):
    order_key, pick_key = jax.random.split(key)
    pair_count = SLOTS // 2
    middle = (jax.random.permutation(pick_key, pair_count - 2) < REPL - 2).astype(jnp.int32)
    marked = jnp.concatenate([jnp.ones((1,), jnp.int32), middle, jnp.ones((1,), jnp.int32)])
    slot_range = jnp.arange(SLOTS, dtype=jnp.int32)
    fresh = 1 - slot_range % 2 * marked[slot_range // 2]
    position = (jnp.cumsum(fresh) - 1).astype(jnp.int32)
    shuffled = jax.random.permutation(order_key, EXPERTS).astype(jnp.int32)
    return shuffled[position]


def draw_slot_expert(key, part):
    return placement_table(key)


def draw_w_gate(key, part):
    table = placement_table(key)
    key = jax.random.fold_in(key, 21)

    def one_slot(expert):
        sub = jax.random.fold_in(key, expert)
        return jax.random.normal(sub, (D, HID), jnp.float32)
    return (jax.vmap(one_slot)(table) * D ** (-0.5)).astype(jnp.bfloat16)


def draw_w_up(key, part):
    table = placement_table(key)
    key = jax.random.fold_in(key, 22)

    def one_slot(expert):
        sub = jax.random.fold_in(key, expert)
        return jax.random.normal(sub, (D, HID), jnp.float32)
    return (jax.vmap(one_slot)(table) * D ** (-0.5)).astype(jnp.bfloat16)


def draw_w_down(key, part):
    table = placement_table(key)
    key = jax.random.fold_in(key, 23)

    def one_slot(expert):
        sub = jax.random.fold_in(key, expert)
        return jax.random.normal(sub, (HID, D), jnp.float32)
    return (jax.vmap(one_slot)(table) * HID ** (-0.5)).astype(jnp.bfloat16)


def shard_levels(stream_key, extent, shards, low, high):
    factor_of = 1.0
    for dim, blocks in shards:
        heights = jax.random.uniform(jax.random.fold_in(jax.random.fold_in(stream_key, 6), dim), (blocks,), jnp.float32, low / len(shards), high / len(shards))
        factor_of = factor_of * jnp.repeat(jnp.exp(heights), extent[dim] // blocks).reshape((-1,) + (1,) * (len(extent) - 1 - dim))
    return factor_of


def shared_out(stream_key, own, number, rows, count, top, reach, skew):
    order = jax.random.permutation(stream_key, count)
    crowded, usual = shares(count, rows * top, reach, skew, True), shares(count, rows * top, reach, skew, False)
    places = jnp.arange(count)

    def named(lengths, offset_by):
        used = int((lengths > 0).sum())
        fixed = max(1, used // 4)
        shifted = fixed + (places - fixed + offset_by * (used - fixed)) % max(1, count - fixed)
        return jnp.zeros((count,), jnp.int32).at[order[jnp.where(places < fixed, places, shifted)]].set(jnp.asarray(lengths, jnp.int32))

    lengths = jnp.where(number % 4 == 0, named(crowded, number // 4), named(usual, number - number // 4 - 1))
    mixed = jax.random.permutation(jax.random.fold_in(own, 3), count)
    giver, receiver = mixed[0:count // 2 * 2:2], mixed[1:count // 2 * 2:2]
    slack = jnp.minimum(lengths[giver] - 1, reach - lengths[receiver]) // 2
    slack = jnp.where((giver == order[0]) | (receiver == order[0]) | (lengths[receiver] == 0), 0, jnp.maximum(slack, 0))
    shifted = jax.random.randint(jax.random.fold_in(own, 4), (count // 2,), 0, 1 << 20) % (slack + 1)
    lengths = lengths.at[giver].add(-shifted).at[receiver].add(shifted)
    labels = jnp.searchsorted(jnp.cumsum(lengths), jnp.arange(rows * top), side="right").astype(jnp.int32)
    listing = labels.reshape(top, rows).T
    listing = listing[jax.random.permutation(jax.random.fold_in(own, 1), rows)]
    offset_by = jax.random.randint(jax.random.fold_in(own, 2), (rows, 1), 0, top)
    return jnp.take_along_axis(listing, (jnp.arange(top)[None, :] + offset_by) % top, axis=1)


def shares(number_of, total, most, skew, full):
    loads = [(1 << 20) // math.isqrt(grade ** skew) + 1 for grade in range(1, number_of + 1)]
    largest = most if full else min(most, max(-(-total // number_of), total * loads[0] // sum(loads)))
    least = 1 if total - largest >= number_of - 1 else 0
    given, rest = [largest] + [least] * (number_of - 1), total - largest - least * (number_of - 1)
    while rest > 0:
        candidates = [i for i in range(1, number_of) if given[i] < largest] or [i for i in range(1, number_of) if given[i] < most]
        mass, left = sum([loads[i] for i in candidates]), rest
        for i in candidates:
            more = min(most - given[i], max(1, left * loads[i] // mass), rest)
            given[i] = given[i] + more
            rest = rest - more
    return np.array(given)


def centred(rng, dims, deviation, bound, cuts=(), kind=jnp.bfloat16):
    drawn = deviation * jax.random.normal(rng, dims, jnp.float32)
    if cuts:
        drawn = drawn * shard_levels(rng, dims, cuts, -0.22, 0.18)
    return jnp.clip(drawn, -bound, bound).astype(kind)


def setup_inputs(seed: int = 0) -> dict:
    splits = jax.random.split(jax.random.key(seed), 9)
    tokens = centred(splits[0], (TOKENS, D), 1.0, 6.0, ((0, 32),))
    cotangent = centred(splits[1], (TOKENS, D), 1.0, 6.0, ((0, 32),))
    expert_ids_keys = jax.random.split(jax.random.fold_in(splits[2], 1), TOKENS // TOK_GRP)
    expert_ids_turns = jax.random.permutation(jax.random.fold_in(splits[2], 3), TOKENS // TOK_GRP)
    expert_ids = jax.vmap(lambda own, number: shared_out(jax.random.fold_in(splits[2], 2), own, number, TOK_GRP, EXPERTS, TOP, CAP, 2))(expert_ids_keys, expert_ids_turns).reshape((TOKENS, TOP))
    gate_probs = jnp.clip(0.049804688 + 0.9501953 * jax.random.uniform(splits[3], (TOKENS, TOP), jnp.float32) ** shard_levels(splits[3], (TOKENS, TOP), ((0, 32),), -0.2, 0.2), 0.049804688, 1.0).astype(jnp.bfloat16)
    slot_expert = draw_slot_expert(jax.random.fold_in(splits[8], 71), 0)
    w_gate = draw_w_gate(jax.random.fold_in(splits[8], 71), 0)
    w_up = draw_w_up(jax.random.fold_in(splits[8], 71), 0)
    w_down = draw_w_down(jax.random.fold_in(splits[8], 71), 0)
    return {"tokens": tokens, "cotangent": cotangent, "expert_ids": expert_ids, "gate_probs": gate_probs, "slot_expert": slot_expert, "w_gate": w_gate, "w_up": w_up, "w_down": w_down}


def silu_parts(gate):
    sig = jax.nn.sigmoid(gate)
    return gate * sig, sig * (1.0 + gate * (1.0 - sig))


def contract(left, right, left_dim, right_dim):
    return lax.dot_general(left, right, (((left_dim,), (right_dim,)), ((), ())), preferred_element_type=jnp.float32)


def reference(tokens, cotangent, expert_ids, gate_probs, slot_expert, w_gate, w_up, w_down):
    assigns = TOKENS * TOP
    most_rows = N_EXPERT * CAP
    block = HID // N_DP
    flat_ids = expert_ids.reshape(assigns)
    x_pad = jnp.concatenate([tokens, jnp.zeros((1, D), tokens.dtype)], axis=0)
    dy_pad = jnp.concatenate([cotangent, jnp.zeros((1, D), cotangent.dtype)], axis=0)
    p_pad = jnp.concatenate([gate_probs.reshape(assigns), jnp.zeros((1,), gate_probs.dtype)], axis=0)

    def one_expert(carry, expert):
        dx_acc, score_acc = carry
        picked = jnp.nonzero(flat_ids == expert, size=most_rows, fill_value=assigns)[0].astype(jnp.int32)
        tok_index = (picked // TOP).astype(jnp.int32)
        xs = x_pad[tok_index]
        dys = dy_pad[tok_index]
        probs = p_pad[picked]
        slot = jnp.argmax((slot_expert == expert).astype(jnp.int32)).astype(jnp.int32)
        wg = w_gate[slot]
        wu = w_up[slot]
        wd = w_down[slot]
        gate = jnp.dot(xs, wg, preferred_element_type=jnp.float32)
        up = jnp.dot(xs, wu, preferred_element_type=jnp.float32)
        act, slope = silu_parts(gate)
        hidden = (act * up).astype(jnp.bfloat16)
        out = jnp.dot(hidden, wd, preferred_element_type=jnp.float32)
        score = jnp.sum(dys.astype(jnp.float32) * out, axis=1)
        d_out = (probs.astype(jnp.float32)[:, None] * dys.astype(jnp.float32)).astype(jnp.bfloat16)
        d_hidden = contract(d_out, wd, 1, 1)
        d_gate_pre = (d_hidden * up * slope).astype(jnp.bfloat16)
        d_up_pre = (d_hidden * act).astype(jnp.bfloat16)
        g_down = contract(hidden, d_out, 0, 0).astype(jnp.bfloat16)
        g_gate = contract(xs, d_gate_pre, 0, 0).astype(jnp.bfloat16)
        g_up = contract(xs, d_up_pre, 0, 0).astype(jnp.bfloat16)
        pieces = jnp.zeros((most_rows, D), jnp.float32)
        for index in range(N_DP):
            lo = index * block
            piece = contract(d_gate_pre[:, lo:lo + block], wg[:, lo:lo + block], 1, 1)
            piece = piece + contract(d_up_pre[:, lo:lo + block], wu[:, lo:lo + block], 1, 1)
            rounded = lax.optimization_barrier(piece.astype(jnp.bfloat16))
            pieces = pieces + rounded.astype(jnp.float32)
        dx_acc = dx_acc.at[tok_index].add(pieces)
        score_acc = score_acc.at[picked].set(score)
        return (dx_acc, score_acc), (g_gate, g_up, g_down)

    start = (jnp.zeros((TOKENS + 1, D), jnp.float32), jnp.zeros((assigns + 1,), jnp.float32))
    (dx_acc, score_acc), (all_gate, all_up, all_down) = lax.scan(one_expert, start, jnp.arange(EXPERTS, dtype=jnp.int32))
    d_tokens = dx_acc[:TOKENS].astype(jnp.bfloat16)
    d_probs = score_acc[:assigns].reshape(TOKENS, TOP)
    return d_tokens, d_probs, all_gate[slot_expert], all_up[slot_expert], all_down[slot_expert]
```

```python
import functools

import jax
import jax.numpy as jnp
from jax import lax
from jax.experimental import pallas as pl
from jax.experimental.pallas import tpu as pltpu
from jax.sharding import PartitionSpec as P

PLANE = 8
LANES = 128
BF16 = jnp.bfloat16
F32 = jnp.float32
VMEM_BYTES = 60 * 1024 * 1024


def silu_parts(gate):
    sig = jax.nn.sigmoid(gate)
    return (gate * sig, sig * (1.0 + gate * (1.0 - sig)))


def contract(left, right, left_dim, right_dim):
    return lax.dot_general(
        left, right, (((left_dim,), (right_dim,)), ((), ())), preferred_element_type=jnp.float32
    )


def column_tile(width):
    return width // 7 if width % (7 * LANES) == 0 else LANES


def remote(src, dst, send_sem, recv_sem, device):
    return pltpu.make_async_remote_copy(
        src_ref=src,
        dst_ref=dst,
        send_sem=send_sem,
        recv_sem=recv_sem,
        device_id={"expert": device},
        device_id_type=pl.DeviceIdType.MESH,
    )


def greet(planes, z, p):
    barrier = pltpu.get_barrier_semaphore()
    for j in range(1, PLANE):
        pl.semaphore_signal(
            barrier,
            inc=1,
            device_id={"expert": z * PLANE + (p + j) % PLANE},
            device_id_type=pl.DeviceIdType.MESH,
        )
    for k in range(1, planes):
        pl.semaphore_signal(
            barrier,
            inc=1,
            device_id={"expert": (z + k) % planes * PLANE + p},
            device_id_type=pl.DeviceIdType.MESH,
        )
    pl.semaphore_wait(barrier, PLANE - 1 + planes - 1)


def one_hot_rows(codes, weights, cap):
    seat = lax.broadcasted_iota(jnp.int32, (cap, codes.shape[1]), 0).astype(F32)
    parts = []
    for q in range(PLANE):
        parts.append(jnp.where(seat == codes[q : q + 1, :], weights[q : q + 1, :], 0.0))
    return jnp.concatenate(parts, axis=0).astype(BF16)


def dispatch_kernel(
    planes, meta_ref, x_ref, dy_ref, rx, rdy, gm_out, gm, gx, gdy, sx, sdy, msend, mrecv,
    zsend, zrecv, psend, precv, lsem
):
    me = lax.axis_index("expert")
    z, p = me // PLANE, me % PLANE
    cap = rx.shape[1]
    width = x_ref.shape[1]
    tile = column_tile(width)
    greet(planes, z, p)

    def meta_copy(k):
        there = (z + k) % planes
        return remote(
            meta_ref.at[there], gm.at[z], msend.at[k], mrecv.at[z], there * PLANE + p
        )

    for k in range(1, planes):
        meta_copy(k).start()

    def chain_copy(which, up, src, ref):
        held = (gx, gdy)[which]
        there = z + 1 if up else z - 1
        return remote(
            ref, held.at[src], zsend.at[which, up, src], zrecv.at[which, src], there * PLANE + p
        )

    def chain_goes(up, src):
        return (src <= z) & (z < planes - 1) if up else (src >= z) & (z > 0)

    def forward(which, src, ref):
        for up in (0, 1):

            @pl.when(chain_goes(up, src))
            def _():
                chain_copy(which, up, src, ref).start()

    def plane_copy(which, src, j):
        packed, out = ((sx, rx), (sdy, rdy))[which]
        q = (p + j) % PLANE
        return remote(
            packed.at[src, q],
            out.at[src * PLANE + p],
            psend.at[which, src, j],
            precv.at[which, src, j],
            z * PLANE + q,
        )

    def own_copy(which, src):
        packed, out = ((sx, rx), (sdy, rdy))[which]
        return pltpu.make_async_copy(
            packed.at[src, p], out.at[src * PLANE + p], lsem.at[which, src]
        )

    def pack(which, src, ref):
        packed = (sx, sdy)[which]
        codes = gm[src, 0:PLANE, :]
        weights = gm[src, PLANE : 2 * PLANE, :] if which else jnp.ones_like(codes)
        rows = one_hot_rows(codes, weights, cap)

        @pl.loop(0, width // tile)
        def _(c):
            cols = pl.ds(pl.multiple_of(c * tile, tile), tile)
            got = jnp.dot(rows, ref[:, cols], preferred_element_type=F32)
            for q in range(PLANE):
                packed[src, q, :, cols] = got[q * cap : (q + 1) * cap].astype(BF16)

        for j in range(1, PLANE):
            plane_copy(which, src, j).start()
        own_copy(which, src).start()

    forward(0, z, x_ref)
    forward(1, z, dy_ref)
    gm[z] = meta_ref[z]
    pack(0, z, x_ref)
    pack(1, z, dy_ref)

    @pl.loop(0, 2 * (planes - 1))
    def _(i):
        away = (i // 2 + 1) * (1 - 2 * (i % 2))
        src = z - away

        @pl.when((src >= 0) & (src < planes))
        def _():
            remote(gm.at[src], gm.at[src], msend.at[0], mrecv.at[src], me).wait_recv()
            for which in (0, 1):
                held = (gx, gdy)[which]
                remote(
                    held.at[src], held.at[src], zsend.at[which, 0, src], zrecv.at[which, src], me
                ).wait_recv()
                forward(which, src, held.at[src])
                pack(which, src, held.at[src])

    gm_out[...] = gm[...]
    for k in range(1, planes):
        meta_copy(k).wait_send()

    @pl.loop(0, planes)
    def _(src):
        for which in (0, 1):
            for up in (0, 1):

                @pl.when(chain_goes(up, src))
                def _():
                    held = (gx, gdy)[which]
                    chain_copy(which, up, src, held.at[src]).wait_send()

            for j in range(1, PLANE):
                copy = plane_copy(which, src, j)
                copy.wait_send()
                copy.wait_recv()
            own_copy(which, src).wait()


def dispatch(meta, tokens, cotangent, slots, cap):
    planes = slots // PLANE
    tok, width = tokens.shape
    vmem = pl.BlockSpec(memory_space=pltpu.VMEM)
    anywhere = pl.BlockSpec(memory_space=pl.ANY)
    return pl.pallas_call(
        functools.partial(dispatch_kernel, planes),
        out_shape=(
            jax.ShapeDtypeStruct((slots, cap, width), BF16),
            jax.ShapeDtypeStruct((slots, cap, width), BF16),
            jax.ShapeDtypeStruct((planes, 2 * PLANE, tok), F32),
        ),
        in_specs=[vmem] * 3,
        out_specs=(anywhere, anywhere, vmem),
        scratch_shapes=[
            pltpu.VMEM((planes, 2 * PLANE, tok), F32),
            pltpu.VMEM((planes, tok, width), BF16),
            pltpu.VMEM((planes, tok, width), BF16),
            pltpu.VMEM((planes, PLANE, cap, width), BF16),
            pltpu.VMEM((planes, PLANE, cap, width), BF16),
            pltpu.SemaphoreType.DMA((planes,)),
            pltpu.SemaphoreType.DMA((planes,)),
            pltpu.SemaphoreType.DMA((2, 2, planes)),
            pltpu.SemaphoreType.DMA((2, planes)),
            pltpu.SemaphoreType.DMA((2, planes, PLANE)),
            pltpu.SemaphoreType.DMA((2, planes, PLANE)),
            pltpu.SemaphoreType.DMA((2, planes)),
        ],
        compiler_params=pltpu.CompilerParams(
            collective_id=0, has_side_effects=True, vmem_limit_bytes=VMEM_BYTES
        ),
    )(meta, tokens, cotangent)


def combine_kernel(
    planes, piece, gm_ref, dx_ref, found_ref, rp, sp, rs, psend, precv, lsem, zsend, zrecv
):
    me = lax.axis_index("expert")
    z, p = me // PLANE, me % PLANE
    cap, wide = piece.shape[1], piece.shape[2]
    width = wide - LANES
    greet(planes, z, p)
    order = sorted(range(planes), key=lambda k: -min(k, planes - k))

    def plane_copy(b, j):
        q = (p + j) % PLANE
        return remote(
            piece.at[b * PLANE + q], rp.at[b, p], psend.at[b, j], precv.at[b, j], z * PLANE + q
        )

    def own_copy(b):
        return pltpu.make_async_copy(piece.at[b * PLANE + p], rp.at[b, p], lsem.at[b])

    def home_copy(b):
        return remote(sp.at[b], rs.at[z], zsend.at[b], zrecv.at[z], b * PLANE + p)

    for k in order:
        b = (z + k) % planes
        for j in range(1, PLANE):
            plane_copy(b, j).start()
        own_copy(b).start()

    def partial(b, rows, cols):
        parts = [rp[b, q, :, cols].astype(F32) for q in range(PLANE)]
        return contract(rows, jnp.concatenate(parts, axis=0).astype(BF16), 0, 0)

    def arrived(b):
        for j in range(1, PLANE):
            plane_copy(b, j).wait_recv()
        own_copy(b).wait()
        codes = gm_ref[b, 0:PLANE, :]
        return one_hot_rows(codes, jnp.ones_like(codes), cap)

    tile = column_tile(width)

    for k in order[:-1]:
        b = (z + k) % planes
        rows = arrived(b)

        @pl.loop(0, width // tile)
        def _(c):
            cols = pl.ds(pl.multiple_of(c * tile, tile), tile)
            sp[b, :, cols] = partial(b, rows, cols).astype(BF16)

        sp[b, :, width:wide] = partial(b, rows, slice(width, wide)).astype(BF16)
        home_copy(b).start()

    own_rows = arrived(z)
    for k in order[:-1]:
        src = (z + k) % planes
        remote(rs.at[src], rs.at[src], zsend.at[src], zrecv.at[src], me).wait_recv()

    def total(cols):
        acc = partial(z, own_rows, cols)
        for k in order[:-1]:
            acc = acc + rs[(z + k) % planes, :, cols].astype(F32)
        return acc

    @pl.loop(0, width // tile)
    def _(c):
        cols = pl.ds(pl.multiple_of(c * tile, tile), tile)
        dx_ref[:, cols] = total(cols).astype(BF16)

    found_ref[...] = total(slice(width, wide))

    for k in order:
        b = (z + k) % planes
        for j in range(1, PLANE):
            plane_copy(b, j).wait_send()
    for k in order[:-1]:
        home_copy((z + k) % planes).wait_send()


def combine(piece, gm, tok):
    slots, cap, wide = piece.shape
    planes = slots // PLANE
    vmem = pl.BlockSpec(memory_space=pltpu.VMEM)
    anywhere = pl.BlockSpec(memory_space=pl.ANY)
    return pl.pallas_call(
        functools.partial(combine_kernel, planes),
        out_shape=(
            jax.ShapeDtypeStruct((tok, wide - LANES), BF16),
            jax.ShapeDtypeStruct((tok, LANES), F32),
        ),
        in_specs=[anywhere, vmem],
        out_specs=(vmem, vmem),
        scratch_shapes=[
            pltpu.VMEM((planes, PLANE, cap, wide), BF16),
            pltpu.VMEM((planes, tok, wide), BF16),
            pltpu.VMEM((planes, tok, wide), BF16),
            pltpu.SemaphoreType.DMA((planes, PLANE)),
            pltpu.SemaphoreType.DMA((planes, PLANE)),
            pltpu.SemaphoreType.DMA((planes,)),
            pltpu.SemaphoreType.DMA((planes,)),
            pltpu.SemaphoreType.DMA((planes,)),
        ],
        compiler_params=pltpu.CompilerParams(
            collective_id=1, has_side_effects=True, vmem_limit_bytes=VMEM_BYTES
        ),
    )(piece, gm)


def shards(tokens, cotangent, expert_ids, gate_probs, slot_expert, w_gate, w_up, w_down):
    slots = lax.axis_size("expert")
    here = lax.axis_index("expert")
    planes = slots // PLANE
    tok_rows, quarter = tokens.shape
    top = expert_ids.shape[1]
    experts = slots - max(2, slots // 8)
    capacity = max(2, 5 * tok_rows * top // (4 * experts))
    capacity = (capacity + 7) // 8 * 8
    width = w_gate.shape[1]
    total = slots * capacity
    hit = expert_ids[:, :, None] == slot_expert[None, None, :]
    probs = gate_probs.astype(F32)
    hits = hit.astype(F32)
    taken = jnp.sum(hits, axis=1)
    weight = jnp.sum(hits * probs[:, :, None], axis=1)
    row = jnp.arange(tok_rows, dtype=jnp.int32)
    earlier = (row[:, None] > row[None, :]).astype(BF16)
    rank = jnp.dot(earlier, taken.astype(BF16), preferred_element_type=F32)
    code = jnp.where(taken > 0.0, rank, -1.0)
    meta = jnp.concatenate(
        [code.T.reshape(planes, PLANE, tok_rows), weight.T.reshape(planes, PLANE, tok_rows)],
        axis=1,
    )
    part_x, part_dy, got_meta = dispatch(meta, tokens, cotangent, slots, capacity)
    xs = lax.all_gather(part_x, "dp", axis=2, tiled=True).reshape(total, width)
    d_out = lax.all_gather(part_dy, "dp", axis=2, tiled=True).reshape(total, width)
    wg = w_gate[0]
    wu = w_up[0]
    wd = w_down[0]
    gate = contract(xs, wg, 1, 0)
    up = contract(xs, wu, 1, 0)
    d_hidden = contract(d_out, wd, 1, 1)
    act, slope = silu_parts(gate)
    hidden = (act * up).astype(BF16)
    score = jnp.sum(hidden.astype(F32) * d_hidden, axis=1)
    d_gate_pre = (d_hidden * up * slope).astype(BF16)
    d_up_pre = (d_hidden * act).astype(BF16)
    piece = contract(d_gate_pre, wg, 1, 1) + contract(d_up_pre, wu, 1, 1)
    summed = lax.psum_scatter(
        piece.astype(BF16).reshape(slots, capacity, width),
        "dp",
        scatter_dimension=2,
        tiled=True,
    )
    scores = lax.psum(score.reshape(slots, capacity), "dp").astype(BF16)
    lane = jnp.arange(LANES, dtype=jnp.int32)
    placed_scores = jnp.where(lane == here, scores[:, :, None], 0.0).astype(BF16)
    slot = jnp.arange(slots, dtype=jnp.int32)
    repeat = (slot_expert[:, None] == slot_expert[None, :]) & (slot[:, None] > slot[None, :])
    first = jnp.logical_not(jnp.any(repeat, axis=1))
    plane_first = lax.dynamic_slice_in_dim(first, here // PLANE * PLANE, PLANE, 0)
    back_code = jnp.where(plane_first[None, :, None], got_meta[:, :PLANE], -1.0)
    d_tokens, found = combine(
        jnp.concatenate([summed, placed_scores], axis=2), back_code, tok_rows
    )
    grad_down = contract(hidden, d_out, 0, 0).astype(BF16)[None]
    grad_gate = contract(xs, d_gate_pre, 0, 0).astype(BF16)[None]
    grad_up = contract(xs, d_up_pre, 0, 0).astype(BF16)[None]
    listed = jnp.where(hit & first[None, None, :], found[:, None, :slots], 0.0)
    d_probs = jnp.sum(listed, axis=2) / probs
    return (d_tokens, d_probs, grad_gate, grad_up, grad_down)


def solution(mesh):
    placed = (
        P("expert", "dp"),
        P("expert", "dp"),
        P("expert", None),
        P("expert", None),
        P(),
        P("expert", None, "dp"),
        P("expert", None, "dp"),
        P("expert", "dp", None),
    )
    return jax.shard_map(
        shards,
        mesh=mesh,
        in_specs=placed,
        out_specs=(
            P("expert", "dp"),
            P("expert", None),
            P("expert", None, "dp"),
            P("expert", None, "dp"),
            P("expert", "dp", None),
        ),
        check_vma=False,
    )
```

```python
import functools

import jax
import jax.numpy as jnp
from jax import lax
from jax.experimental import pallas as pl
from jax.experimental.pallas import tpu as pltpu
from jax.sharding import PartitionSpec as P

PLANE = 8
LANES = 128
BF16 = jnp.bfloat16
F32 = jnp.float32
VMEM_BYTES = 62 * 1024 * 1024


def silu_parts(gate):
    sig = jax.nn.sigmoid(gate)
    return (gate * sig, sig * (1.0 + gate * (1.0 - sig)))


def contract(left, right, left_dim, right_dim):
    return lax.dot_general(
        left, right, (((left_dim,), (right_dim,)), ((), ())), preferred_element_type=jnp.float32
    )


def column_tile(width):
    return width // 7 if width % (7 * LANES) == 0 else LANES


def remote(src, dst, send_sem, recv_sem, device):
    return pltpu.make_async_remote_copy(
        src_ref=src,
        dst_ref=dst,
        send_sem=send_sem,
        recv_sem=recv_sem,
        device_id={"expert": device},
        device_id_type=pl.DeviceIdType.MESH,
    )


def greet(planes, z, p):
    barrier = pltpu.get_barrier_semaphore()
    for j in range(1, PLANE):
        pl.semaphore_signal(
            barrier,
            inc=1,
            device_id={"expert": z * PLANE + (p + j) % PLANE},
            device_id_type=pl.DeviceIdType.MESH,
        )
    for k in range(1, planes):
        pl.semaphore_signal(
            barrier,
            inc=1,
            device_id={"expert": (z + k) % planes * PLANE + p},
            device_id_type=pl.DeviceIdType.MESH,
        )
    pl.semaphore_wait(barrier, PLANE - 1 + planes - 1)


def one_hot_rows(codes, weights, cap):
    seat = lax.broadcasted_iota(jnp.int32, (cap, codes.shape[1]), 0).astype(F32)
    parts = []
    for q in range(PLANE):
        parts.append(jnp.where(seat == codes[q : q + 1, :], weights[q : q + 1, :], 0.0))
    return jnp.concatenate(parts, axis=0).astype(BF16)


def gather_rows(ref, lead, cols):
    parts = [ref[lead * PLANE + q, :, cols].astype(F32) for q in range(PLANE)]
    return jnp.concatenate(parts, axis=0).astype(BF16)


def dispatch_kernel(planes, fused, *refs):
    if fused:
        meta_ref, x_ref, dy_ref, wg_hbm, wu_hbm, wd_hbm = refs[:6]
        ox, ody, gm_out, hid_out, dg_out, du_out, sc_out = refs[6:13]
        gm, gx, gdy, sx, sdy, rx, rdy, wg, wu, wd = refs[13:23]
        acc_g, acc_u, acc_h, st_hid, st_dg, st_du, st_sc = refs[23:30]
        msend, mrecv, zsend, zrecv, psend, precv, lsem, wsem, osem, dsem, xsem = refs[30:]
    else:
        meta_ref, x_ref, dy_ref, rx, rdy, gm_out, gm, gx, gdy, sx, sdy = refs[:11]
        msend, mrecv, zsend, zrecv, psend, precv, lsem, xsem = refs[11:]
    me = lax.axis_index("expert")
    z, p = me // PLANE, me % PLANE
    cap = rx.shape[1]
    width = x_ref.shape[1]
    tile = column_tile(width)
    block = PLANE * cap

    def in_copy(which):
        return pltpu.make_async_copy(
            (x_ref, dy_ref)[which], (gx, gdy)[which].at[z], xsem.at[which]
        )

    def weight_copy(k):
        return pltpu.make_async_copy(
            (wg_hbm, wu_hbm, wd_hbm)[k], (wg, wu, wd)[k], wsem.at[k]
        )

    in_copy(0).start()
    in_copy(1).start()
    greet(planes, z, p)

    def meta_copy(k):
        there = (z + k) % planes
        return remote(
            meta_ref.at[there], gm.at[z], msend.at[k], mrecv.at[z], there * PLANE + p
        )

    for k in range(1, planes):
        meta_copy(k).start()

    def chain_copy(which, up, src, ref):
        held = (gx, gdy)[which]
        there = z + 1 if up else z - 1
        return remote(
            ref, held.at[src], zsend.at[which, up, src], zrecv.at[which, src], there * PLANE + p
        )

    def chain_goes(up, src):
        return (src <= z) & (z < planes - 1) if up else (src >= z) & (z > 0)

    def forward(which, src, ref):
        for up in (0, 1):

            @pl.when(chain_goes(up, src))
            def _():
                chain_copy(which, up, src, ref).start()

    def plane_copy(which, src, j):
        packed, out = ((sx, rx), (sdy, rdy))[which]
        q = (p + j) % PLANE
        return remote(
            packed.at[src, q],
            out.at[src * PLANE + p],
            psend.at[which, src, j],
            precv.at[which, src, j],
            z * PLANE + q,
        )

    def own_copy(which, src):
        packed, out = ((sx, rx), (sdy, rdy))[which]
        return pltpu.make_async_copy(
            packed.at[src, p], out.at[src * PLANE + p], lsem.at[which, src]
        )

    def pack(which, src):
        ref, packed = ((gx, sx), (gdy, sdy))[which]
        codes = gm[src, 0:PLANE, :]
        weights = gm[src, PLANE : 2 * PLANE, :] if which else jnp.ones_like(codes)
        rows = one_hot_rows(codes, weights, cap)

        @pl.loop(0, width // tile)
        def _(c):
            cols = pl.ds(pl.multiple_of(c * tile, tile), tile)
            got = jnp.dot(rows, ref[src, :, cols], preferred_element_type=F32)
            for q in range(PLANE):
                packed[src, q, :, cols] = got[q * cap : (q + 1) * cap].astype(BF16)

        for j in range(1, PLANE):
            plane_copy(which, src, j).start()
        own_copy(which, src).start()

    def arrived(which, src):
        for j in range(1, PLANE):
            plane_copy(which, src, j).wait_recv()
        own_copy(which, src).wait()

    def row_copy(which, src):
        got, out = ((rx, ox), (rdy, ody))[which]
        blocks = pl.ds(src * PLANE, PLANE)
        return pltpu.make_async_copy(got.at[blocks], out.at[blocks], osem.at[which, src])

    def stage_copies(src):
        rows = pl.ds(pl.multiple_of(src * block, block), block)
        pairs = ((st_hid, hid_out), (st_dg, dg_out), (st_du, du_out), (st_sc, sc_out))
        return [
            pltpu.make_async_copy(held, out.at[rows], dsem.at[k])
            for k, (held, out) in enumerate(pairs)
        ]

    def compute(src, opening):
        arrived(0, src)
        row_copy(0, src).start()
        if opening:
            for k in range(3):
                weight_copy(k).wait()
        acc_g[...] = jnp.zeros_like(acc_g)
        acc_u[...] = jnp.zeros_like(acc_u)
        acc_h[...] = jnp.zeros_like(acc_h)

        @pl.loop(0, width // tile)
        def _(c):
            cols = pl.ds(pl.multiple_of(c * tile, tile), tile)
            rows = gather_rows(rx, src, cols)
            acc_g[...] += jnp.dot(rows, wg[cols, :], preferred_element_type=F32)
            acc_u[...] += jnp.dot(rows, wu[cols, :], preferred_element_type=F32)

        arrived(1, src)
        row_copy(1, src).start()

        @pl.loop(0, width // tile)
        def _(c):
            cols = pl.ds(pl.multiple_of(c * tile, tile), tile)
            acc_h[...] += contract(gather_rows(rdy, src, cols), wd[:, cols], 1, 1)

        if not opening:
            for copy in stage_copies(src):
                copy.wait()
        share = acc_g.shape[1]
        part = share // 4

        def slice_step(c, score):
            cols = pl.ds(pl.multiple_of(c * part, part), part)
            act, slope = silu_parts(acc_g[:, cols])
            up = acc_u[:, cols]
            d_hidden = acc_h[:, cols]
            hidden = (act * up).astype(BF16)
            st_hid[:, cols] = hidden
            st_dg[:, cols] = (d_hidden * up * slope).astype(BF16)
            st_du[:, cols] = (d_hidden * act).astype(BF16)
            return score + jnp.sum(hidden.astype(F32) * d_hidden, axis=1, keepdims=True)

        score = lax.fori_loop(0, 4, slice_step, jnp.zeros((block, 1), F32))
        lane = lax.broadcasted_iota(jnp.int32, (block, LANES), 1)
        st_sc[...] = jnp.where(lane == me, score, 0.0).astype(BF16)
        for copy in stage_copies(src):
            copy.start()

    forward(0, z, x_ref)
    forward(1, z, dy_ref)
    if fused:
        for k in range(3):
            weight_copy(k).start()
    gm[z] = meta_ref[z]
    for which in (0, 1):
        in_copy(which).wait()
        pack(which, z)

    def valid(src, dist):
        return (src >= 0) & (src < planes)

    def exchange_step(dist):
        for which in (0, 1):
            held = (gx, gdy)[which]
            for src in (z - dist, z + dist):

                @pl.when(valid(src, dist))
                def _():
                    remote(
                        held.at[src], held.at[src], zsend.at[which, 0, src],
                        zrecv.at[which, src], me
                    ).wait_recv()
                    forward(which, src, held.at[src])

        for src in (z - dist, z + dist):

            @pl.when(valid(src, dist))
            def _():
                remote(gm.at[src], gm.at[src], msend.at[0], mrecv.at[src], me).wait_recv()
                pack(0, src)
                pack(1, src)

    def compute_step(dist):
        for src in (z - dist, z + dist):

            @pl.when(valid(src, dist))
            def _():
                compute(src, False)

    exchange_step(1)
    if fused:
        compute(z, True)

    @pl.loop(2, planes)
    def _(dist):
        exchange_step(dist)
        if fused:
            compute_step(dist - 1)

    if fused:
        compute_step(planes - 1)
        for copy in stage_copies(z):
            copy.wait()

    gm_out[...] = gm[...]
    for k in range(1, planes):
        meta_copy(k).wait_send()

    @pl.loop(0, planes)
    def _(src):
        for which in (0, 1):
            for up in (0, 1):

                @pl.when(chain_goes(up, src))
                def _():
                    held = (gx, gdy)[which]
                    chain_copy(which, up, src, held.at[src]).wait_send()

            for j in range(1, PLANE):
                plane_copy(which, src, j).wait_send()
            if fused:
                row_copy(which, src).wait()
            else:
                arrived(which, src)


def dispatch(meta, tokens, cotangent, slots, cap, weights):
    planes = slots // PLANE
    tok, width = tokens.shape
    fused = weights is not None
    vmem = pl.BlockSpec(memory_space=pltpu.VMEM)
    anywhere = pl.BlockSpec(memory_space=pl.ANY)
    rows = jax.ShapeDtypeStruct((slots, cap, width), BF16)
    dma = pltpu.SemaphoreType.DMA
    out_shape = [rows, rows, jax.ShapeDtypeStruct((planes, 2 * PLANE, tok), F32)]
    out_specs = [anywhere, anywhere, vmem]
    scratch = [
        pltpu.VMEM((planes, 2 * PLANE, tok), F32),
        pltpu.VMEM((planes, tok, width), BF16),
        pltpu.VMEM((planes, tok, width), BF16),
        pltpu.VMEM((planes, PLANE, cap, width), BF16),
        pltpu.VMEM((planes, PLANE, cap, width), BF16),
    ]
    sems = [
        dma((planes,)),
        dma((planes,)),
        dma((2, 2, planes)),
        dma((2, planes)),
        dma((2, planes, PLANE)),
        dma((2, planes, PLANE)),
        dma((2, planes)),
    ]
    args = [meta, tokens, cotangent]
    if fused:
        share = weights[0].shape[1]
        block = PLANE * cap
        for columns in (share, share, share, LANES):
            out_shape.append(jax.ShapeDtypeStruct((slots * cap, columns), BF16))
            out_specs.append(anywhere)
        scratch += [pltpu.VMEM((slots, cap, width), BF16)] * 2
        scratch += [pltpu.VMEM(w.shape, BF16) for w in weights]
        scratch += [pltpu.VMEM((block, share), F32)] * 3
        scratch += [pltpu.VMEM((block, share), BF16)] * 3 + [pltpu.VMEM((block, LANES), BF16)]
        sems += [dma((3,)), dma((2, planes)), dma((4,))]
        args += list(weights)
    sems += [dma((2,))]
    return pl.pallas_call(
        functools.partial(dispatch_kernel, planes, fused),
        out_shape=out_shape,
        in_specs=[vmem] + [anywhere] * (len(args) - 1),
        out_specs=out_specs,
        scratch_shapes=scratch + sems,
        compiler_params=pltpu.CompilerParams(
            collective_id=0, has_side_effects=True, vmem_limit_bytes=VMEM_BYTES
        ),
    )(*args)


def combine_kernel(planes, fused, *refs):
    if fused:
        dg_ref, du_ref, sc_ref, wg_hbm, wu_hbm, gm_ref, dx_ref, found_ref = refs[:8]
        piece, wg, wu, rp, sp, rs, psend, precv, lsem, zsend, zrecv, wsem = refs[8:]
    else:
        piece, gm_ref, dx_ref, found_ref = refs[:4]
        rp, sp, rs, psend, precv, lsem, zsend, zrecv = refs[4:]
    me = lax.axis_index("expert")
    z, p = me // PLANE, me % PLANE
    cap, wide = piece.shape[1], piece.shape[2]
    width = wide - LANES
    tile = column_tile(width)
    block = PLANE * cap

    def weight_copy(k, c):
        rows = pl.ds(pl.multiple_of(c * tile, tile), tile)
        return pltpu.make_async_copy(
            (wg_hbm, wu_hbm)[k].at[rows], (wg, wu)[k].at[rows], wsem.at[k, c]
        )

    if fused:
        for c in range(width // tile):
            weight_copy(0, c).start()
            weight_copy(1, c).start()
    greet(planes, z, p)

    low = jnp.where(z < planes // 2, z, planes - 1 - z)

    def dest(i):
        if i == planes - 1:
            return z
        b = jnp.where(i < planes - 1 - low, planes - 1 - i, i - (planes - 1 - low))
        return jnp.where(z < planes // 2, b, planes - 1 - b)

    def plane_copy(b, j):
        q = (p + j) % PLANE
        return remote(
            piece.at[b * PLANE + q], rp.at[b, p], psend.at[b, j], precv.at[b, j], z * PLANE + q
        )

    def own_copy(b):
        return pltpu.make_async_copy(piece.at[b * PLANE + p], rp.at[b, p], lsem.at[b])

    def chain_copy(b, up):
        there = z + 1 if up else z - 1
        slot = b if up else jnp.where(b == there, planes, b)
        return remote(sp.at[b], rs.at[slot], zsend.at[b], zrecv.at[slot], there * PLANE + p)

    def make_piece(b, opening):
        if not fused:
            return
        rows = pl.ds(pl.multiple_of(b * block, block), block)

        @pl.loop(0, width // tile)
        def _(c):
            if opening:
                weight_copy(0, c).wait()
                weight_copy(1, c).wait()
            cols = pl.ds(pl.multiple_of(c * tile, tile), tile)
            got = contract(dg_ref[rows, :], wg[cols, :], 1, 1)
            got = got + contract(du_ref[rows, :], wu[cols, :], 1, 1)
            for q in range(PLANE):
                piece[b * PLANE + q, :, cols] = got[q * cap : (q + 1) * cap].astype(BF16)

        score = sc_ref[rows, :].astype(F32)
        for q in range(PLANE):
            piece[b * PLANE + q, :, width:wide] = score[q * cap : (q + 1) * cap].astype(BF16)

    def send_piece(b):
        for j in range(1, PLANE):
            plane_copy(b, j).start()
        own_copy(b).start()

    def partial(b, rows, cols):
        parts = [rp[b, q, :, cols].astype(F32) for q in range(PLANE)]
        return contract(rows, jnp.concatenate(parts, axis=0).astype(BF16), 0, 0)

    def arrived(b):
        for j in range(1, PLANE):
            plane_copy(b, j).wait_recv()
        own_copy(b).wait()
        codes = gm_ref[b, 0:PLANE, :]
        return one_hot_rows(codes, jnp.ones_like(codes), cap)

    def wait_sum(slot):
        remote(rs.at[slot], rs.at[slot], zsend.at[0], zrecv.at[slot], me).wait_recv()

    def each(body):
        @pl.loop(0, width // tile)
        def _(c):
            body(pl.ds(pl.multiple_of(c * tile, tile), tile))

        body(slice(width, wide))

    make_piece(dest(0), True)
    send_piece(dest(0))
    for i in range(planes - 1):
        b = dest(i)
        make_piece(dest(i + 1), False)
        rows = arrived(b)
        send_piece(dest(i + 1))
        begins = ((b > z) & (z == 0)) | ((b < z) & (z == planes - 1))

        @pl.when(begins)
        def _():
            def start(cols):
                sp[b, :, cols] = partial(b, rows, cols).astype(BF16)

            each(start)

        @pl.when(jnp.logical_not(begins))
        def _():
            wait_sum(b)

            def add(cols):
                sp[b, :, cols] = (partial(b, rows, cols) + rs[b, :, cols].astype(F32)).astype(BF16)

            each(add)

        @pl.when(b > z)
        def _():
            chain_copy(b, 1).start()

        @pl.when(b < z)
        def _():
            chain_copy(b, 0).start()

    own_rows = arrived(z)

    @pl.when(z > 0)
    def _():
        wait_sum(z)

    @pl.when(z < planes - 1)
    def _():
        wait_sum(planes)

    @pl.when(z == 0)
    def _():
        rs[0] = jnp.zeros_like(rs[0])

    @pl.when(z == planes - 1)
    def _():
        rs[planes] = jnp.zeros_like(rs[planes])

    def total(cols):
        acc = partial(z, own_rows, cols) + rs[z, :, cols].astype(F32)
        return acc + rs[planes, :, cols].astype(F32)

    @pl.loop(0, width // tile)
    def _(c):
        cols = pl.ds(pl.multiple_of(c * tile, tile), tile)
        dx_ref[:, cols] = total(cols).astype(BF16)

    found_ref[...] = total(slice(width, wide))

    @pl.loop(0, planes)
    def _(b):
        for j in range(1, PLANE):
            plane_copy(b, j).wait_send()

        @pl.when(b > z)
        def _():
            chain_copy(b, 1).wait_send()

        @pl.when(b < z)
        def _():
            chain_copy(b, 0).wait_send()


def combine(parts, gm, slots, cap, tok, width):
    planes = slots // PLANE
    wide = width + LANES
    fused = len(parts) > 1
    vmem = pl.BlockSpec(memory_space=pltpu.VMEM)
    anywhere = pl.BlockSpec(memory_space=pl.ANY)
    dma = pltpu.SemaphoreType.DMA
    scratch = [
        pltpu.VMEM((planes, PLANE, cap, wide), BF16),
        pltpu.VMEM((planes, tok, wide), BF16),
        pltpu.VMEM((planes + 1, tok, wide), BF16),
    ]
    sems = [
        dma((planes, PLANE)),
        dma((planes, PLANE)),
        dma((planes,)),
        dma((planes,)),
        dma((planes + 1,)),
    ]
    in_specs = [anywhere, vmem]
    if fused:
        scratch = [
            pltpu.VMEM((slots, cap, wide), BF16),
            pltpu.VMEM(parts[3].shape, BF16),
            pltpu.VMEM(parts[4].shape, BF16),
        ] + scratch
        sems += [dma((2, width // column_tile(width)))]
        in_specs = [vmem] * 3 + [anywhere] * 2 + [vmem]
    return pl.pallas_call(
        functools.partial(combine_kernel, planes, fused),
        out_shape=(
            jax.ShapeDtypeStruct((tok, width), BF16),
            jax.ShapeDtypeStruct((tok, LANES), F32),
        ),
        in_specs=in_specs,
        out_specs=(vmem, vmem),
        scratch_shapes=scratch + sems,
        compiler_params=pltpu.CompilerParams(
            collective_id=1, has_side_effects=True, vmem_limit_bytes=VMEM_BYTES
        ),
    )(*parts, gm)


def shards(tokens, cotangent, expert_ids, gate_probs, slot_expert, w_gate, w_up, w_down):
    slots = lax.axis_size("expert")
    here = lax.axis_index("expert")
    planes = slots // PLANE
    tok_rows, quarter = tokens.shape
    top = expert_ids.shape[1]
    experts = slots - max(2, slots // 8)
    capacity = max(2, 5 * tok_rows * top // (4 * experts))
    capacity = (capacity + 7) // 8 * 8
    width = w_gate.shape[1]
    total = slots * capacity
    hit = expert_ids[:, :, None] == slot_expert[None, None, :]
    probs = gate_probs.astype(F32)
    hits = hit.astype(F32)
    taken = jnp.sum(hits, axis=1)
    weight = jnp.sum(hits * probs[:, :, None], axis=1)
    row = jnp.arange(tok_rows, dtype=jnp.int32)
    earlier = (row[:, None] > row[None, :]).astype(BF16)
    rank = jnp.dot(earlier, taken.astype(BF16), preferred_element_type=F32)
    code = jnp.where(taken > 0.0, rank, -1.0)
    meta = jnp.concatenate(
        [code.T.reshape(planes, PLANE, tok_rows), weight.T.reshape(planes, PLANE, tok_rows)],
        axis=1,
    )
    wg = w_gate[0]
    wu = w_up[0]
    wd = w_down[0]
    slot = jnp.arange(slots, dtype=jnp.int32)
    repeat = (slot_expert[:, None] == slot_expert[None, :]) & (slot[:, None] > slot[None, :])
    first = jnp.logical_not(jnp.any(repeat, axis=1))
    plane_first = lax.dynamic_slice_in_dim(first, here // PLANE * PLANE, PLANE, 0)
    fused = lax.axis_size("dp") == 1
    if fused:
        part_x, part_dy, got_meta, hidden, d_gate_pre, d_up_pre, placed_scores = dispatch(
            meta, tokens, cotangent, slots, capacity, (wg, wu, wd)
        )
        xs = part_x.reshape(total, width)
        d_out = part_dy.reshape(total, width)
        parts = (d_gate_pre, d_up_pre, placed_scores, wg, wu)
    else:
        part_x, part_dy, got_meta = dispatch(meta, tokens, cotangent, slots, capacity, None)
        xs = lax.all_gather(part_x, "dp", axis=2, tiled=True).reshape(total, width)
        d_out = lax.all_gather(part_dy, "dp", axis=2, tiled=True).reshape(total, width)
        gate = contract(xs, wg, 1, 0)
        up = contract(xs, wu, 1, 0)
        d_hidden = contract(d_out, wd, 1, 1)
        act, slope = silu_parts(gate)
        hidden = (act * up).astype(BF16)
        score = jnp.sum(hidden.astype(F32) * d_hidden, axis=1)
        d_gate_pre = (d_hidden * up * slope).astype(BF16)
        d_up_pre = (d_hidden * act).astype(BF16)
        piece = contract(d_gate_pre, wg, 1, 1) + contract(d_up_pre, wu, 1, 1)
        summed = lax.psum_scatter(
            piece.astype(BF16).reshape(slots, capacity, width),
            "dp",
            scatter_dimension=2,
            tiled=True,
        )
        scores = lax.psum(score.reshape(slots, capacity), "dp").astype(BF16)
        lane = jnp.arange(LANES, dtype=jnp.int32)
        placed_scores = jnp.where(lane == here, scores[:, :, None], 0.0).astype(BF16)
        parts = (jnp.concatenate([summed, placed_scores], axis=2),)
    back_code = jnp.where(plane_first[None, :, None], got_meta[:, :PLANE], -1.0)
    d_tokens, found = combine(parts, back_code, slots, capacity, tok_rows, quarter)
    grad_down = contract(hidden, d_out, 0, 0).astype(BF16)[None]
    grad_gate = contract(xs, d_gate_pre, 0, 0).astype(BF16)[None]
    grad_up = contract(xs, d_up_pre, 0, 0).astype(BF16)[None]
    listed = jnp.where(hit & first[None, None, :], found[:, None, :slots], 0.0)
    d_probs = jnp.sum(listed, axis=2) / probs
    return (d_tokens, d_probs, grad_gate, grad_up, grad_down)


def solution(mesh):
    placed = (
        P("expert", "dp"),
        P("expert", "dp"),
        P("expert", None),
        P("expert", None),
        P(),
        P("expert", None, "dp"),
        P("expert", None, "dp"),
        P("expert", "dp", None),
    )
    return jax.shard_map(
        shards,
        mesh=mesh,
        in_specs=placed,
        out_specs=(
            P("expert", "dp"),
            P("expert", None),
            P("expert", None, "dp"),
            P("expert", None, "dp"),
            P("expert", "dp", None),
        ),
        check_vma=False,
    )
```

```python
import functools

import jax
import jax.numpy as jnp
from jax import lax
from jax.experimental import pallas as pl
from jax.experimental.pallas import tpu as pltpu
from jax.sharding import PartitionSpec as P

PLANE = 8
LANES = 128
BF16 = jnp.bfloat16
F32 = jnp.float32
VMEM_BYTES = 62 * 1024 * 1024


def silu_parts(gate):
    sig = jax.nn.sigmoid(gate)
    return (gate * sig, sig * (1.0 + gate * (1.0 - sig)))


def contract(left, right, left_dim, right_dim):
    return lax.dot_general(
        left, right, (((left_dim,), (right_dim,)), ((), ())), preferred_element_type=jnp.float32
    )


def column_tile(width):
    return width // 7 if width % (7 * LANES) == 0 else LANES


def remote(src, dst, send_sem, recv_sem, device):
    return pltpu.make_async_remote_copy(
        src_ref=src,
        dst_ref=dst,
        send_sem=send_sem,
        recv_sem=recv_sem,
        device_id={"expert": device},
        device_id_type=pl.DeviceIdType.MESH,
    )


def greet(planes, z, p):
    barrier = pltpu.get_barrier_semaphore()
    for j in range(1, PLANE):
        pl.semaphore_signal(
            barrier,
            inc=1,
            device_id={"expert": z * PLANE + (p + j) % PLANE},
            device_id_type=pl.DeviceIdType.MESH,
        )
    for k in range(1, planes):
        pl.semaphore_signal(
            barrier,
            inc=1,
            device_id={"expert": (z + k) % planes * PLANE + p},
            device_id_type=pl.DeviceIdType.MESH,
        )
    pl.semaphore_wait(barrier, PLANE - 1 + planes - 1)


def one_hot_rows(codes, weights, cap):
    seat = lax.broadcasted_iota(jnp.int32, (cap, codes.shape[1]), 0).astype(F32)
    parts = []
    for q in range(PLANE):
        parts.append(jnp.where(seat == codes[q : q + 1, :], weights[q : q + 1, :], 0.0))
    return jnp.concatenate(parts, axis=0).astype(BF16)


def gather_rows(ref, lead, cols):
    parts = [ref[lead * PLANE + q, :, cols].astype(F32) for q in range(PLANE)]
    return jnp.concatenate(parts, axis=0).astype(BF16)


def dispatch_kernel(planes, fused, *refs):
    if fused:
        meta_ref, x_ref, dy_ref, wg_hbm, wu_hbm, wd_hbm = refs[:6]
        ox, ody, gm_out, hid_out, dg_out, du_out, sc_out = refs[6:13]
        gm, gx, gdy, sx, sdy, rx, rdy, wg, wu, wd = refs[13:23]
        acc_g, acc_u, acc_h, st_hid, st_dg, st_du, st_sc = refs[23:30]
        msend, mrecv, zsend, zrecv, psend, precv, lsem, wsem, osem, dsem, xsem = refs[30:]
    else:
        meta_ref, x_ref, dy_ref, rx, rdy, gm_out, gm, gx, gdy, sx, sdy = refs[:11]
        msend, mrecv, zsend, zrecv, psend, precv, lsem, xsem = refs[11:]
    me = lax.axis_index("expert")
    z, p = me // PLANE, me % PLANE
    cap = rx.shape[1]
    width = x_ref.shape[1]
    tile = column_tile(width)
    block = PLANE * cap

    def in_copy(which):
        return pltpu.make_async_copy(
            (x_ref, dy_ref)[which], (gx, gdy)[which].at[z], xsem.at[which]
        )

    def weight_copy(k):
        return pltpu.make_async_copy(
            (wg_hbm, wu_hbm, wd_hbm)[k], (wg, wu, wd)[k], wsem.at[k]
        )

    in_copy(0).start()
    in_copy(1).start()
    greet(planes, z, p)

    def meta_copy(k):
        there = (z + k) % planes
        return remote(
            meta_ref.at[there], gm.at[z], msend.at[k], mrecv.at[z], there * PLANE + p
        )

    for k in range(1, planes):
        meta_copy(k).start()

    def chain_copy(which, up, src, ref):
        held = (gx, gdy)[which]
        there = z + 1 if up else z - 1
        return remote(
            ref, held.at[src], zsend.at[which, up, src], zrecv.at[which, src], there * PLANE + p
        )

    def chain_goes(up, src):
        return (src <= z) & (z < planes - 1) if up else (src >= z) & (z > 0)

    def forward(which, src, ref):
        for up in (0, 1):

            @pl.when(chain_goes(up, src))
            def _():
                chain_copy(which, up, src, ref).start()

    def plane_copy(which, src, j):
        packed, out = ((sx, rx), (sdy, rdy))[which]
        q = (p + j) % PLANE
        return remote(
            packed.at[src, q],
            out.at[src * PLANE + p],
            psend.at[which, src, j],
            precv.at[which, src, j],
            z * PLANE + q,
        )

    def own_copy(which, src):
        packed, out = ((sx, rx), (sdy, rdy))[which]
        return pltpu.make_async_copy(
            packed.at[src, p], out.at[src * PLANE + p], lsem.at[which, src]
        )

    def pack(which, src):
        ref, packed = ((gx, sx), (gdy, sdy))[which]
        codes = gm[src, 0:PLANE, :]
        weights = gm[src, PLANE : 2 * PLANE, :] if which else jnp.ones_like(codes)
        rows = one_hot_rows(codes, weights, cap)

        @pl.loop(0, width // tile)
        def _(c):
            cols = pl.ds(pl.multiple_of(c * tile, tile), tile)
            got = jnp.dot(rows, ref[src, :, cols], preferred_element_type=F32)
            for q in range(PLANE):
                packed[src, q, :, cols] = got[q * cap : (q + 1) * cap].astype(BF16)

        for j in range(1, PLANE):
            plane_copy(which, src, j).start()
        own_copy(which, src).start()

    def arrived(which, src):
        for j in range(1, PLANE):
            plane_copy(which, src, j).wait_recv()
        own_copy(which, src).wait()

    def row_copy(which, src):
        got, out = ((rx, ox), (rdy, ody))[which]
        blocks = pl.ds(src * PLANE, PLANE)
        return pltpu.make_async_copy(got.at[blocks], out.at[blocks], osem.at[which, src])

    def stage_copies(src):
        rows = pl.ds(pl.multiple_of(src * block, block), block)
        pairs = ((st_hid, hid_out), (st_dg, dg_out), (st_du, du_out), (st_sc, sc_out))
        return [
            pltpu.make_async_copy(held, out.at[rows], dsem.at[k])
            for k, (held, out) in enumerate(pairs)
        ]

    def compute(src, opening):
        arrived(0, src)
        row_copy(0, src).start()
        if opening:
            for k in range(3):
                weight_copy(k).wait()
        acc_g[...] = jnp.zeros_like(acc_g)
        acc_u[...] = jnp.zeros_like(acc_u)
        acc_h[...] = jnp.zeros_like(acc_h)

        @pl.loop(0, width // tile)
        def _(c):
            cols = pl.ds(pl.multiple_of(c * tile, tile), tile)
            rows = gather_rows(rx, src, cols)
            acc_g[...] += jnp.dot(rows, wg[cols, :], preferred_element_type=F32)
            acc_u[...] += jnp.dot(rows, wu[cols, :], preferred_element_type=F32)

        arrived(1, src)
        row_copy(1, src).start()

        @pl.loop(0, width // tile)
        def _(c):
            cols = pl.ds(pl.multiple_of(c * tile, tile), tile)
            acc_h[...] += contract(gather_rows(rdy, src, cols), wd[:, cols], 1, 1)

        if not opening:
            for copy in stage_copies(src):
                copy.wait()
        share = acc_g.shape[1]
        part = share // 4

        def slice_step(c, score):
            cols = pl.ds(pl.multiple_of(c * part, part), part)
            act, slope = silu_parts(acc_g[:, cols])
            up = acc_u[:, cols]
            d_hidden = acc_h[:, cols]
            hidden = (act * up).astype(BF16)
            st_hid[:, cols] = hidden
            st_dg[:, cols] = (d_hidden * up * slope).astype(BF16)
            st_du[:, cols] = (d_hidden * act).astype(BF16)
            return score + jnp.sum(hidden.astype(F32) * d_hidden, axis=1, keepdims=True)

        score = lax.fori_loop(0, 4, slice_step, jnp.zeros((block, 1), F32))
        lane = lax.broadcasted_iota(jnp.int32, (block, LANES), 1)
        st_sc[...] = jnp.where(lane == me, score, 0.0).astype(BF16)
        for copy in stage_copies(src):
            copy.start()

    def valid(src):
        return (src >= 0) & (src < planes)

    def take(which, dist):
        held = (gx, gdy)[which]
        for src in (z - dist, z + dist):

            @pl.when(valid(src))
            def _():
                remote(
                    held.at[src], held.at[src], zsend.at[which, 0, src], zrecv.at[which, src], me
                ).wait_recv()
                forward(which, src, held.at[src])

    def pack_step(which, dist):
        for src in (z - dist, z + dist):

            @pl.when(valid(src))
            def _():
                if which == 0:
                    remote(gm.at[src], gm.at[src], msend.at[0], mrecv.at[src], me).wait_recv()
                pack(which, src)

    def compute_step(dist):
        for src in (z - dist, z + dist):

            @pl.when(valid(src))
            def _():
                compute(src, False)

    forward(0, z, x_ref)
    if fused:
        for k in range(3):
            weight_copy(k).start()
    gm[z] = meta_ref[z]
    in_copy(0).wait()
    in_copy(1).wait()
    pack(0, z)
    for up in (0, 1):

        @pl.when(chain_goes(up, z))
        def _():
            chain_copy(0, up, z, x_ref).wait_send()

    forward(1, z, dy_ref)
    take(0, 1)
    pack(1, z)
    pack_step(0, 1)

    def stage(dist, last):
        take(1, dist)
        if not last:
            take(0, dist + 1)
        pack_step(1, dist)
        if not last:
            pack_step(0, dist + 1)

    if planes > 2:
        stage(1, False)
        if fused:
            compute(z, True)

        @pl.loop(2, planes - 1)
        def _(dist):
            stage(dist, False)
            if fused:
                compute_step(dist - 1)

        stage(planes - 1, True)
        if fused:
            compute_step(planes - 2)
    else:
        stage(1, True)
        if fused:
            compute(z, True)

    if fused:
        compute_step(planes - 1)
        for copy in stage_copies(z):
            copy.wait()

    gm_out[...] = gm[...]
    for k in range(1, planes):
        meta_copy(k).wait_send()

    @pl.loop(0, planes)
    def _(src):
        for which in (0, 1):
            for up in (0, 1):

                unmet = chain_goes(up, src) & (src != z) if which == 0 else chain_goes(up, src)

                @pl.when(unmet)
                def _():
                    held = (gx, gdy)[which]
                    chain_copy(which, up, src, held.at[src]).wait_send()

            for j in range(1, PLANE):
                plane_copy(which, src, j).wait_send()
            if fused:
                row_copy(which, src).wait()
            else:
                arrived(which, src)


def dispatch(meta, tokens, cotangent, slots, cap, weights):
    planes = slots // PLANE
    tok, width = tokens.shape
    fused = weights is not None
    vmem = pl.BlockSpec(memory_space=pltpu.VMEM)
    anywhere = pl.BlockSpec(memory_space=pl.ANY)
    rows = jax.ShapeDtypeStruct((slots, cap, width), BF16)
    dma = pltpu.SemaphoreType.DMA
    out_shape = [rows, rows, jax.ShapeDtypeStruct((planes, 2 * PLANE, tok), F32)]
    out_specs = [anywhere, anywhere, vmem]
    scratch = [
        pltpu.VMEM((planes, 2 * PLANE, tok), F32),
        pltpu.VMEM((planes, tok, width), BF16),
        pltpu.VMEM((planes, tok, width), BF16),
        pltpu.VMEM((planes, PLANE, cap, width), BF16),
        pltpu.VMEM((planes, PLANE, cap, width), BF16),
    ]
    sems = [
        dma((planes,)),
        dma((planes,)),
        dma((2, 2, planes)),
        dma((2, planes)),
        dma((2, planes, PLANE)),
        dma((2, planes, PLANE)),
        dma((2, planes)),
    ]
    args = [meta, tokens, cotangent]
    if fused:
        share = weights[0].shape[1]
        block = PLANE * cap
        for columns in (share, share, share, LANES):
            out_shape.append(jax.ShapeDtypeStruct((slots * cap, columns), BF16))
            out_specs.append(anywhere)
        scratch += [pltpu.VMEM((slots, cap, width), BF16)] * 2
        scratch += [pltpu.VMEM(w.shape, BF16) for w in weights]
        scratch += [pltpu.VMEM((block, share), F32)] * 3
        scratch += [pltpu.VMEM((block, share), BF16)] * 3 + [pltpu.VMEM((block, LANES), BF16)]
        sems += [dma((3,)), dma((2, planes)), dma((4,))]
        args += list(weights)
    sems += [dma((2,))]
    return pl.pallas_call(
        functools.partial(dispatch_kernel, planes, fused),
        out_shape=out_shape,
        in_specs=[vmem] + [anywhere] * (len(args) - 1),
        out_specs=out_specs,
        scratch_shapes=scratch + sems,
        compiler_params=pltpu.CompilerParams(
            collective_id=0, has_side_effects=True, vmem_limit_bytes=VMEM_BYTES
        ),
    )(*args)


def combine_kernel(planes, fused, *refs):
    if fused:
        dg_ref, du_ref, sc_ref, wg_hbm, wu_hbm, gm_ref, dx_ref, found_ref = refs[:8]
        piece, wg, wu, rp, sp, rs, psend, precv, lsem, zsend, zrecv, wsem = refs[8:]
    else:
        piece, gm_ref, dx_ref, found_ref = refs[:4]
        rp, sp, rs, psend, precv, lsem, zsend, zrecv = refs[4:]
    me = lax.axis_index("expert")
    z, p = me // PLANE, me % PLANE
    cap, wide = piece.shape[1], piece.shape[2]
    width = wide - LANES
    tile = column_tile(width)
    block = PLANE * cap

    def weight_copy(k, c):
        rows = pl.ds(pl.multiple_of(c * tile, tile), tile)
        return pltpu.make_async_copy(
            (wg_hbm, wu_hbm)[k].at[rows], (wg, wu)[k].at[rows], wsem.at[k, c]
        )

    if fused:
        for c in range(width // tile):
            weight_copy(0, c).start()
            weight_copy(1, c).start()
    greet(planes, z, p)

    low = jnp.where(z < planes // 2, z, planes - 1 - z)

    def dest(i):
        if i == planes - 1:
            return z
        b = jnp.where(i < planes - 1 - low, planes - 1 - i, i - (planes - 1 - low))
        return jnp.where(z < planes // 2, b, planes - 1 - b)

    def plane_copy(b, j):
        q = (p + j) % PLANE
        return remote(
            piece.at[b * PLANE + q], rp.at[b, p], psend.at[b, j], precv.at[b, j], z * PLANE + q
        )

    def own_copy(b):
        return pltpu.make_async_copy(piece.at[b * PLANE + p], rp.at[b, p], lsem.at[b])

    def chain_copy(b, up):
        there = z + 1 if up else z - 1
        slot = b if up else jnp.where(b == there, planes, b)
        return remote(sp.at[b], rs.at[slot], zsend.at[b], zrecv.at[slot], there * PLANE + p)

    def make_piece(b, opening):
        if not fused:
            return
        rows = pl.ds(pl.multiple_of(b * block, block), block)

        @pl.loop(0, width // tile)
        def _(c):
            if opening:
                weight_copy(0, c).wait()
                weight_copy(1, c).wait()
            cols = pl.ds(pl.multiple_of(c * tile, tile), tile)
            got = contract(dg_ref[rows, :], wg[cols, :], 1, 1)
            got = got + contract(du_ref[rows, :], wu[cols, :], 1, 1)
            for q in range(PLANE):
                piece[b * PLANE + q, :, cols] = got[q * cap : (q + 1) * cap].astype(BF16)

        score = sc_ref[rows, :].astype(F32)
        for q in range(PLANE):
            piece[b * PLANE + q, :, width:wide] = score[q * cap : (q + 1) * cap].astype(BF16)

    def send_piece(b):
        for j in range(1, PLANE):
            plane_copy(b, j).start()
        own_copy(b).start()

    def partial(b, rows, cols):
        parts = [rp[b, q, :, cols].astype(F32) for q in range(PLANE)]
        return contract(rows, jnp.concatenate(parts, axis=0).astype(BF16), 0, 0)

    def arrived(b):
        for j in range(1, PLANE):
            plane_copy(b, j).wait_recv()
        own_copy(b).wait()
        codes = gm_ref[b, 0:PLANE, :]
        return one_hot_rows(codes, jnp.ones_like(codes), cap)

    def wait_sum(slot):
        remote(rs.at[slot], rs.at[slot], zsend.at[0], zrecv.at[slot], me).wait_recv()

    def each(body):
        @pl.loop(0, width // tile)
        def _(c):
            body(pl.ds(pl.multiple_of(c * tile, tile), tile))

        body(slice(width, wide))

    make_piece(dest(0), True)
    send_piece(dest(0))
    for i in range(planes - 1):
        b = dest(i)
        make_piece(dest(i + 1), False)
        rows = arrived(b)
        send_piece(dest(i + 1))
        begins = ((b > z) & (z == 0)) | ((b < z) & (z == planes - 1))

        @pl.when(begins)
        def _():
            def start(cols):
                sp[b, :, cols] = partial(b, rows, cols).astype(BF16)

            each(start)

        @pl.when(jnp.logical_not(begins))
        def _():
            wait_sum(b)

            def add(cols):
                sp[b, :, cols] = (partial(b, rows, cols) + rs[b, :, cols].astype(F32)).astype(BF16)

            each(add)

        @pl.when(b > z)
        def _():
            chain_copy(b, 1).start()

        @pl.when(b < z)
        def _():
            chain_copy(b, 0).start()

    own_rows = arrived(z)

    @pl.when(z > 0)
    def _():
        wait_sum(z)

    @pl.when(z < planes - 1)
    def _():
        wait_sum(planes)

    @pl.when(z == 0)
    def _():
        rs[0] = jnp.zeros_like(rs[0])

    @pl.when(z == planes - 1)
    def _():
        rs[planes] = jnp.zeros_like(rs[planes])

    def total(cols):
        acc = partial(z, own_rows, cols) + rs[z, :, cols].astype(F32)
        return acc + rs[planes, :, cols].astype(F32)

    @pl.loop(0, width // tile)
    def _(c):
        cols = pl.ds(pl.multiple_of(c * tile, tile), tile)
        dx_ref[:, cols] = total(cols).astype(BF16)

    found_ref[...] = total(slice(width, wide))

    @pl.loop(0, planes)
    def _(b):
        for j in range(1, PLANE):
            plane_copy(b, j).wait_send()

        @pl.when(b > z)
        def _():
            chain_copy(b, 1).wait_send()

        @pl.when(b < z)
        def _():
            chain_copy(b, 0).wait_send()


def combine(parts, gm, slots, cap, tok, width):
    planes = slots // PLANE
    wide = width + LANES
    fused = len(parts) > 1
    vmem = pl.BlockSpec(memory_space=pltpu.VMEM)
    anywhere = pl.BlockSpec(memory_space=pl.ANY)
    dma = pltpu.SemaphoreType.DMA
    scratch = [
        pltpu.VMEM((planes, PLANE, cap, wide), BF16),
        pltpu.VMEM((planes, tok, wide), BF16),
        pltpu.VMEM((planes + 1, tok, wide), BF16),
    ]
    sems = [
        dma((planes, PLANE)),
        dma((planes, PLANE)),
        dma((planes,)),
        dma((planes,)),
        dma((planes + 1,)),
    ]
    in_specs = [anywhere, vmem]
    if fused:
        scratch = [
            pltpu.VMEM((slots, cap, wide), BF16),
            pltpu.VMEM(parts[3].shape, BF16),
            pltpu.VMEM(parts[4].shape, BF16),
        ] + scratch
        sems += [dma((2, width // column_tile(width)))]
        in_specs = [vmem] * 3 + [anywhere] * 2 + [vmem]
    return pl.pallas_call(
        functools.partial(combine_kernel, planes, fused),
        out_shape=(
            jax.ShapeDtypeStruct((tok, width), BF16),
            jax.ShapeDtypeStruct((tok, LANES), F32),
        ),
        in_specs=in_specs,
        out_specs=(vmem, vmem),
        scratch_shapes=scratch + sems,
        compiler_params=pltpu.CompilerParams(
            collective_id=1, has_side_effects=True, vmem_limit_bytes=VMEM_BYTES
        ),
    )(*parts, gm)


def grads_kernel(xs, d_out, hidden, d_gate, d_up, g_gate, g_up, g_down, hidden_t):
    @pl.when(pl.program_id(0) == 0)
    def _():
        hidden_t[...] = hidden[...].T

    xs_t = xs[...].T
    g_gate[...] = jnp.dot(xs_t, d_gate[...], preferred_element_type=F32).astype(BF16)
    g_up[...] = jnp.dot(xs_t, d_up[...], preferred_element_type=F32).astype(BF16)
    g_down[...] = jnp.dot(hidden_t[...], d_out[...], preferred_element_type=F32).astype(BF16)


def weight_grads(xs, d_out, hidden, d_gate, d_up):
    rows, width = xs.shape
    share = hidden.shape[1]
    tile = column_tile(width)
    whole = pl.BlockSpec((rows, share), lambda i: (0, 0))
    piece = pl.BlockSpec((rows, tile), lambda i: (0, i))
    across = pl.BlockSpec((tile, share), lambda i: (i, 0))
    return pl.pallas_call(
        grads_kernel,
        grid=(width // tile,),
        out_shape=(
            jax.ShapeDtypeStruct((width, share), BF16),
            jax.ShapeDtypeStruct((width, share), BF16),
            jax.ShapeDtypeStruct((share, width), BF16),
        ),
        in_specs=[piece, piece, whole, whole, whole],
        out_specs=(across, across, pl.BlockSpec((share, tile), lambda i: (0, i))),
        scratch_shapes=[pltpu.VMEM((share, rows), BF16)],
        compiler_params=pltpu.CompilerParams(vmem_limit_bytes=VMEM_BYTES),
    )(xs, d_out, hidden, d_gate, d_up)


def shards(tokens, cotangent, expert_ids, gate_probs, slot_expert, w_gate, w_up, w_down):
    slots = lax.axis_size("expert")
    here = lax.axis_index("expert")
    planes = slots // PLANE
    tok_rows, quarter = tokens.shape
    top = expert_ids.shape[1]
    experts = slots - max(2, slots // 8)
    capacity = max(2, 5 * tok_rows * top // (4 * experts))
    capacity = (capacity + 7) // 8 * 8
    width = w_gate.shape[1]
    total = slots * capacity
    hit = expert_ids[:, :, None] == slot_expert[None, None, :]
    probs = gate_probs.astype(F32)
    hits = hit.astype(F32)
    taken = jnp.sum(hits, axis=1)
    weight = jnp.sum(hits * probs[:, :, None], axis=1)
    row = jnp.arange(tok_rows, dtype=jnp.int32)
    earlier = (row[:, None] > row[None, :]).astype(BF16)
    rank = jnp.dot(earlier, taken.astype(BF16), preferred_element_type=F32)
    code = jnp.where(taken > 0.0, rank, -1.0)
    meta = jnp.concatenate(
        [code.T.reshape(planes, PLANE, tok_rows), weight.T.reshape(planes, PLANE, tok_rows)],
        axis=1,
    )
    wg = w_gate[0]
    wu = w_up[0]
    wd = w_down[0]
    slot = jnp.arange(slots, dtype=jnp.int32)
    repeat = (slot_expert[:, None] == slot_expert[None, :]) & (slot[:, None] > slot[None, :])
    first = jnp.logical_not(jnp.any(repeat, axis=1))
    plane_first = lax.dynamic_slice_in_dim(first, here // PLANE * PLANE, PLANE, 0)
    fused = lax.axis_size("dp") == 1
    if fused:
        part_x, part_dy, got_meta, hidden, d_gate_pre, d_up_pre, placed_scores = dispatch(
            meta, tokens, cotangent, slots, capacity, (wg, wu, wd)
        )
        xs = part_x.reshape(total, width)
        d_out = part_dy.reshape(total, width)
        parts = (d_gate_pre, d_up_pre, placed_scores, wg, wu)
    else:
        part_x, part_dy, got_meta = dispatch(meta, tokens, cotangent, slots, capacity, None)
        xs = lax.all_gather(part_x, "dp", axis=2, tiled=True).reshape(total, width)
        d_out = lax.all_gather(part_dy, "dp", axis=2, tiled=True).reshape(total, width)
        gate = contract(xs, wg, 1, 0)
        up = contract(xs, wu, 1, 0)
        d_hidden = contract(d_out, wd, 1, 1)
        act, slope = silu_parts(gate)
        hidden = (act * up).astype(BF16)
        score = jnp.sum(hidden.astype(F32) * d_hidden, axis=1)
        d_gate_pre = (d_hidden * up * slope).astype(BF16)
        d_up_pre = (d_hidden * act).astype(BF16)
        piece = contract(d_gate_pre, wg, 1, 1) + contract(d_up_pre, wu, 1, 1)
        summed = lax.psum_scatter(
            piece.astype(BF16).reshape(slots, capacity, width),
            "dp",
            scatter_dimension=2,
            tiled=True,
        )
        scores = lax.psum(score.reshape(slots, capacity), "dp").astype(BF16)
        lane = jnp.arange(LANES, dtype=jnp.int32)
        placed_scores = jnp.where(lane == here, scores[:, :, None], 0.0).astype(BF16)
        parts = (jnp.concatenate([summed, placed_scores], axis=2),)
    back_code = jnp.where(plane_first[None, :, None], got_meta[:, :PLANE], -1.0)
    d_tokens, found = combine(parts, back_code, slots, capacity, tok_rows, quarter)
    grad_gate, grad_up, grad_down = weight_grads(xs, d_out, hidden, d_gate_pre, d_up_pre)
    listed = jnp.where(hit & first[None, None, :], found[:, None, :slots], 0.0)
    d_probs = jnp.sum(listed, axis=2) / probs
    return (d_tokens, d_probs, grad_gate[None], grad_up[None], grad_down[None])


def solution(mesh):
    placed = (
        P("expert", "dp"),
        P("expert", "dp"),
        P("expert", None),
        P("expert", None),
        P(),
        P("expert", None, "dp"),
        P("expert", None, "dp"),
        P("expert", "dp", None),
    )
    return jax.shard_map(
        shards,
        mesh=mesh,
        in_specs=placed,
        out_specs=(
            P("expert", "dp"),
            P("expert", None),
            P("expert", None, "dp"),
            P("expert", None, "dp"),
            P("expert", "dp", None),
        ),
        check_vma=False,
    )
```
